32 devices in a mesh: groups: 2 (over y), leaf: 16 (over z, x, core).
Axes of the slice: x: 2, y: 2, z: 4, core: 2. Of those that a mesh axis runs over, the one named last changes fastest.
Arguments:
- rhs: bfloat16 [64, 32768], P('groups', 'leaf'), parts along dimension 0, may hold values from -6 to 6
- bases: bfloat16 [512, 32, 128], P(('groups', 'leaf')), parts along dimension 0, may hold values from -0.5 to 0.5
- transfers: bfloat16 [512, 32, 32], P(('groups', 'leaf')), parts along dimension 0, may hold values from -0.5 to 0.5
- near_slots: int32 [32, 8, 8, 2], P(('groups', 'leaf')), parts along dimension 0, may hold values from -1 to 15, as said below
- near_blocks: bfloat16 [32, 8, 8, 128, 128], P(('groups', 'leaf')), parts along dimension 0, may hold values from -0.078125 to 0.078125
- local_pairs: int32 [32, 288, 2], P(('groups', 'leaf')), parts along dimension 0, may hold values from 0 to 15
- local_blocks: bfloat16 [32, 288, 128, 128], P(('groups', 'leaf')), parts along dimension 0, may hold values from -0.078125 to 0.078125
- far_slots: int32 [32, 8, 2, 2], P(('groups', 'leaf')), parts along dimension 0, may hold values from -1 to 15, as said below
- far_blocks: bfloat16 [32, 8, 2, 32, 32], P(('groups', 'leaf')), parts along dimension 0, may hold values from -0.75 to 0.75
- parent_pairs: int32 [32, 4], P(('groups', 'leaf')), parts along dimension 0, may hold values from -1 to 15, as said below
- parent_blocks: bfloat16 [32, 4, 32, 32], P(('groups', 'leaf')), parts along dimension 0, may hold values from -0.25 to 0.25
Outputs:
- first: bfloat16 [64, 32768], P('groups', 'leaf'), parts along dimension 0
- second: bfloat16 [64, 32768], P('groups', 'leaf'), parts along dimension 0
The draws below stay inside these ranges and needn't reach their ends.
There are 2 independent parts, one for each index of `groups`. The reference program is written for one: setup_inputs(seed, part) draws one part's arguments, and reference() takes and returns one part's arrays. A program takes and returns all parts, laid end to end along the dimension named above; each array names one. Nothing has to cross between parts.
Inputs may be any that keep to these rules, and one draw needn't show every extreme that they name: near_slots[d, k, c] concerns neighbour k of owner d: entry 0 is owner d's local target leaf and entry 1 the neighbour's local source leaf, both -1 for an empty slot and for every neighbour outside 0 to 15; on every owner one existing neighbour fills all 8 slots. far_slots[d, k, c] concerns neighbour k of owner d in the same way, both entries -1 for an empty slot and for every neighbour outside 0 to 15; on every owner one existing neighbour fills all 2 slots. `parent_pairs`: the partner owner of each stored parent coupling block, -1 for an empty slot.
All inputs are finite; a program needn't handle non-finite values.
Results may differ from the reference program's by a relative error of at most 0.0065.
Values may be sent and summed in bfloat16 or wider, within the bound.
A program may use at most 128 MiB of HBM per device.

```python
import jax
import jax.numpy as jnp
from jax import lax

LEAF_DEV = 16
P_SIZE = 128
RANK = 32
RHS = 32
NEIGH = 8
CAP = 8
FCAP = 2
PCAP = 4
LOC = 288
OWNERS = 16
LEAVES = 256
PANELS = 32768
N_LEAF = 16


def slot_table(key, slot_count):
    subkeys = jax.random.split(key, 5)
    half = NEIGH // 2
    steps = jnp.arange(NEIGH, dtype=jnp.int32)
    offsets = jnp.where(steps < half, steps - half, steps - half + 1)[None, :, None]
    owner = jnp.arange(OWNERS, dtype=jnp.int32)[:, None, None]
    peer = owner + offsets
    valid = (peer >= 0) & (peer < OWNERS)
    live_rate = jax.random.randint(subkeys[0], (OWNERS, 1, 1), 1, 5)
    draw_roll = jax.random.randint(subkeys[1], (OWNERS, NEIGH, slot_count), 0, 4)
    full_pick = jax.random.randint(subkeys[2], (OWNERS, 1, 1), 0, NEIGH)
    full_step = jnp.where(full_pick < half, full_pick - half, full_pick - half + 1)
    full_valid = (owner + full_step >= 0) & (owner + full_step < OWNERS)
    full_index = jnp.where(full_valid, full_pick, NEIGH - 1 - full_pick)
    is_live = ((draw_roll < live_rate) | (steps[None, :, None] == full_index)) & valid
    target = jax.random.randint(subkeys[3], (OWNERS, NEIGH, slot_count), 0, LEAF_DEV)
    source = jax.random.randint(subkeys[4], (OWNERS, NEIGH, slot_count), 0, LEAF_DEV)
    return jnp.stack([jnp.where(is_live, target, -1), jnp.where(is_live, source, -1)], axis=-1).astype(jnp.int32)


def draw_near_slots(key, part):
    key = jax.random.fold_in(key, 11)
    return slot_table(key, CAP)


def draw_far_slots(key, part):
    key = jax.random.fold_in(key, 12)
    return slot_table(key, FCAP)


def draw_parent_pairs(key, part):
    key = jax.random.fold_in(key, 13)
    subkeys = jax.random.split(key, 3)
    live_rate = jax.random.randint(subkeys[0], (OWNERS, 1), 1, 5)
    draw_roll = jax.random.randint(subkeys[1], (OWNERS, PCAP), 0, 4)
    partner = jax.random.randint(subkeys[2], (OWNERS, PCAP), 0, OWNERS)
    return jnp.where(draw_roll < live_rate, partner, -1).astype(jnp.int32)


def touch_ends(array, key, least, high):
    longest = array.shape.index(max(array.shape))
    spots = []
    for shift in (0, 1):
        where = [jax.random.randint(jax.random.fold_in(key, axis), (), 0, length) for axis, length in enumerate(array.shape)]
        where[longest] = (where[longest] + shift) % array.shape[longest]
        spots.append(tuple(where))
    return array.at[spots[0]].set(least).at[spots[1]].set(high)


def level_of(rng, dims, shards, least, high):
    loudness, own = 1.0, jax.random.fold_in(rng, 6)
    for dim, blocks in shards:
        heights = jnp.exp(jax.random.uniform(jax.random.fold_in(own, dim), (blocks,), jnp.float32, least / len(shards), high / len(shards)))
        loudness = loudness * jnp.repeat(heights, dims[dim] // blocks).reshape([-1 if axis == dim else 1 for axis in range(len(dims))])
    return loudness


def normal_values(stream_key, extent, deviation, most, cuts=(), kind=jnp.bfloat16):
    array = deviation * jax.random.normal(stream_key, extent, jnp.float32)
    if cuts:
        array = array * level_of(stream_key, extent, cuts, -0.22, 0.18)
    return jnp.clip(array, -most, most).astype(kind)


def setup_inputs(seed: int = 0, part: int = 0) -> dict:
    splits = jax.random.split(jax.random.key(seed), 12)
    part_splits = jax.random.split(jax.random.fold_in(splits[11], part), 12)
    rhs = normal_values(part_splits[0], (RHS, PANELS), 1.0, 6.0, ((1, 16),))
    bases = normal_values(part_splits[1], (LEAVES, RANK, P_SIZE), P_SIZE ** -0.5, 0.5, ((0, 16),))
    transfers = normal_values(part_splits[2], (LEAVES, RANK, RANK), (4 * RANK) ** -0.5, 0.5, ((0, 16),))
    near_slots = draw_near_slots(jax.random.fold_in(jax.random.fold_in(splits[11], part), 71), part)
    near_blocks = normal_values(part_splits[4], (OWNERS, NEIGH, CAP, P_SIZE, P_SIZE), (2 * P_SIZE * (LOC + NEIGH * CAP) // LEAF_DEV) ** -0.5, 0.078125, ((0, 16),))
    local_pairs = touch_ends(jax.random.randint(part_splits[5], (OWNERS, LOC, 2), 0, LEAF_DEV), jax.random.fold_in(part_splits[5], 1), 0, LEAF_DEV - 1).astype(jnp.int32)
    local_blocks = normal_values(part_splits[6], (OWNERS, LOC, P_SIZE, P_SIZE), (2 * P_SIZE * (LOC + NEIGH * CAP) // LEAF_DEV) ** -0.5, 0.078125, ((0, 16),))
    far_slots = draw_far_slots(jax.random.fold_in(jax.random.fold_in(splits[11], part), 71), part)
    far_blocks = normal_values(part_splits[8], (OWNERS, NEIGH, FCAP, RANK, RANK), (2 * RANK * NEIGH * FCAP // LEAF_DEV) ** -0.5, 0.75, ((0, 16),))
    parent_pairs = draw_parent_pairs(jax.random.fold_in(jax.random.fold_in(splits[11], part), 71), part)
    parent_blocks = normal_values(part_splits[10], (OWNERS, PCAP, RANK, RANK), (RANK * PCAP * LEAF_DEV // 4) ** -0.5, 0.25, ((0, 16),))
    return {"rhs": rhs, "bases": bases, "transfers": transfers, "near_slots": near_slots, "near_blocks": near_blocks, "local_pairs": local_pairs, "local_blocks": local_blocks, "far_slots": far_slots, "far_blocks": far_blocks, "parent_pairs": parent_pairs, "parent_blocks": parent_blocks}


def neighbour_steps():
    steps = jnp.arange(NEIGH, dtype=jnp.int32)
    half = NEIGH // 2
    return jnp.where(steps < half, steps - half, steps - half + 1).astype(jnp.int32)


def apply_operator(field_now, bases, transfers, near_slots, near_blocks, local_pairs, local_blocks, far_slots, far_blocks, parent_pairs, parent_blocks):
    leaves = N_LEAF * LEAF_DEV
    field_wide = field_now.astype(jnp.float32)
    bases_wide = bases.astype(jnp.float32)
    trans_wide = transfers.astype(jnp.float32)
    coef = jnp.einsum("lap,lrp->lar", bases_wide, field_wide).astype(jnp.bfloat16)
    coef_wide = lax.optimization_barrier(coef).astype(jnp.float32)
    trans_owner = trans_wide.reshape(N_LEAF, LEAF_DEV, RANK, RANK)
    parent = jnp.einsum("dlab,dlbr->dar", trans_owner, coef_wide.reshape(N_LEAF, LEAF_DEV, RANK, RHS)).astype(jnp.bfloat16)
    parent_wide = lax.optimization_barrier(parent).astype(jnp.float32)
    owner_ids = jnp.arange(N_LEAF, dtype=jnp.int32)
    offsets = neighbour_steps()

    def sweep(carry_sums, scan_item):
        near_sum, far_sum = carry_sums
        owner, slots, tiles, pairs, local_tiles, fslots, ftiles = scan_item
        base = owner * LEAF_DEV
        peer_base = (jnp.clip(owner + offsets, 0, N_LEAF - 1) * LEAF_DEV).astype(jnp.int32)
        safe_slots = jnp.maximum(slots, 0).astype(jnp.int32)
        target = base + safe_slots[:, :, 0]
        source = peer_base[:, None] + safe_slots[:, :, 1]
        live_mask = (slots[:, :, 0] >= 0).astype(jnp.float32)[:, :, None, None]
        tile_wide = tiles.astype(jnp.float32)
        into_target = jnp.einsum("pcrq,pcqk->pcrk", field_wide[source], tile_wide) * live_mask
        into_source = jnp.einsum("pcrk,pcqk->pcrq", field_wide[target], tile_wide) * live_mask
        into_source = lax.optimization_barrier(into_source.astype(jnp.bfloat16)).astype(jnp.float32)
        near_sum = near_sum.at[target.reshape(-1)].add(into_target.reshape(-1, RHS, P_SIZE))
        near_sum = near_sum.at[source.reshape(-1)].add(into_source.reshape(-1, RHS, P_SIZE))
        local_target = base + pairs[:, 0].astype(jnp.int32)
        local_source = base + pairs[:, 1].astype(jnp.int32)
        local_wide = local_tiles.astype(jnp.float32)
        near_sum = near_sum.at[local_target].add(jnp.einsum("krq,kqm->krm", field_wide[local_source], local_wide))
        near_sum = near_sum.at[local_source].add(jnp.einsum("krm,kqm->krq", field_wide[local_target], local_wide))
        safe_far = jnp.maximum(fslots, 0).astype(jnp.int32)
        far_target = base + safe_far[:, :, 0]
        far_source = peer_base[:, None] + safe_far[:, :, 1]
        far_mask = (fslots[:, :, 0] >= 0).astype(jnp.float32)[:, :, None, None]
        coupling = ftiles.astype(jnp.float32) * far_mask
        far_into_target = jnp.einsum("pcab,pcbr->pcar", coupling, coef_wide[far_source])
        far_into_source = jnp.einsum("pcab,pcar->pcbr", coupling, coef_wide[far_target])
        far_into_source = lax.optimization_barrier(far_into_source.astype(jnp.bfloat16)).astype(jnp.float32)
        far_sum = far_sum.at[far_target.reshape(-1)].add(far_into_target.reshape(-1, RANK, RHS))
        far_sum = far_sum.at[far_source.reshape(-1)].add(far_into_source.reshape(-1, RANK, RHS))
        return (near_sum, far_sum), None

    start = (jnp.zeros((leaves, RHS, P_SIZE), jnp.float32), jnp.zeros((leaves, RANK, RHS), jnp.float32))
    (near_sum, far_sum), _ = lax.scan(sweep, start, (owner_ids, near_slots, near_blocks, local_pairs, local_blocks, far_slots, far_blocks))
    parent_mask = (parent_pairs >= 0).astype(jnp.float32)[:, :, None, None]
    partner = jnp.maximum(parent_pairs, 0).astype(jnp.int32)
    parent_mats = parent_blocks.astype(jnp.float32) * parent_mask
    own_part = jnp.einsum("djab,djbr->dar", parent_mats, parent_wide[partner])
    returned = jnp.einsum("djab,dar->djbr", parent_mats, parent_wide)
    parent_sum = own_part.at[partner.reshape(-1)].add(returned.reshape(-1, RANK, RHS))
    parent_half = lax.optimization_barrier(parent_sum.astype(jnp.bfloat16)).astype(jnp.float32)
    lifted = jnp.einsum("dlab,dar->dlbr", trans_owner, parent_half).reshape(leaves, RANK, RHS)
    down_half = lax.optimization_barrier((far_sum + lifted).astype(jnp.bfloat16)).astype(jnp.float32)
    result = near_sum + jnp.einsum("lar,lap->lrp", down_half, bases_wide)
    return result.astype(jnp.bfloat16)


def reference(rhs, bases, transfers, near_slots, near_blocks, local_pairs, local_blocks, far_slots, far_blocks, parent_pairs, parent_blocks):
    leaves = N_LEAF * LEAF_DEV
    field_now = rhs.reshape(RHS, leaves, P_SIZE).transpose(1, 0, 2)
    extra = (bases, transfers, near_slots, near_blocks, local_pairs, local_blocks, far_slots, far_blocks, parent_pairs, parent_blocks)
    first_leaf = apply_operator(field_now, *extra)
    second_leaf = apply_operator(first_leaf, *extra)
    first = first_leaf.transpose(1, 0, 2).reshape(RHS, leaves * P_SIZE)
    second = second_leaf.transpose(1, 0, 2).reshape(RHS, leaves * P_SIZE)
    return first, second
```

```python
import jax
import jax.numpy as jnp
from jax import lax
from jax.experimental import pallas as pl
from jax.experimental.pallas import tpu as pltpu
from jax.sharding import PartitionSpec as P

F32 = jnp.float32
BF16 = jnp.bfloat16
NN = (((1,), (0,)), ((), ()))
NT = (((1,), (1,)), ((), ()))
TN = (((0,), (0,)), ((), ()))


def mm(a, b, dims=NN):
    return lax.dot_general(a, b, dims, preferred_element_type=F32)


def shifted(shard, axis, by):
    size = lax.axis_size(axis)
    pairs = [(i, i + by) for i in range(size) if 0 <= i + by < size]
    return lax.ppermute(shard, axis, pairs)


def neighbour_offsets(count):
    half = count // 2
    return [step - half if step < half else step - half + 1 for step in range(count)]


def vmem():
    return pl.BlockSpec(memory_space=pltpu.VMEM)


def smem():
    return pl.BlockSpec(memory_space=pltpu.SMEM)


def leaf_cols(ref, leaf, width):
    return ref[:, pl.ds(pl.multiple_of(leaf * width, width), width)]


def params():
    return pltpu.CompilerParams(vmem_limit_bytes=40 * 1024 * 1024)


def start_kernel(x_ref, bases_ref, transfers_ref, v_ref, u_ref):
    leaves, _, width = bases_ref.shape
    for leaf in range(leaves):
        v_ref[:, leaf * width : (leaf + 1) * width] = mm(
            transfers_ref[leaf], bases_ref[leaf]
        ).astype(BF16)
    u_ref[...] = mm(x_ref[...], v_ref[...], NT).astype(BF16)


def start_call(x, bases, transfers):
    rank = bases.shape[1]
    return pl.pallas_call(
        start_kernel,
        out_shape=(
            jax.ShapeDtypeStruct((rank, x.shape[1]), BF16),
            jax.ShapeDtypeStruct((x.shape[0], rank), BF16),
        ),
        in_specs=[vmem()] * 3,
        out_specs=(vmem(), vmem()),
        compiler_params=params(),
        cost_estimate=pl.CostEstimate(flops=10**7, bytes_accessed=10**6, transcendentals=0),
        name="parent_basis",
    )(x, bases, transfers)


def local_kernel(unroll, pairs_ref, x_ref, blocks_ref, out_ref, *accs):
    step = pl.program_id(0)
    per_step, width = blocks_ref.shape[0], blocks_ref.shape[1]

    @pl.when(step == 0)
    def _():
        for acc in accs:
            acc[...] = jnp.zeros_like(acc)

    def group(i, carry):
        base = i * unroll
        work = []
        for j in range(unroll):
            place = (step * per_step + base + j) * 2
            target, source = pairs_ref[place], pairs_ref[place + 1]
            block = blocks_ref[base + j]
            work.append(
                (
                    target,
                    source,
                    mm(leaf_cols(x_ref, source, width), block),
                    mm(leaf_cols(x_ref, target, width), block, NT),
                )
            )
        for j, (target, source, to_target, to_source) in enumerate(work):
            first, second = accs[2 * (j % 2)], accs[2 * (j % 2) + 1]
            first[target] += to_target
            second[source] += to_source
        return carry

    lax.fori_loop(0, per_step // unroll, group, 0)

    @pl.when(step == pl.num_programs(0) - 1)
    def _():
        out_ref[...] = (accs[0][...] + accs[1][...]) + (accs[2][...] + accs[3][...])


def local_call(x, pairs, blocks):
    count, width = blocks.shape[0], blocks.shape[1]
    leaves = x.shape[1] // width
    steps = next(s for s in (6, 4, 3, 2, 1) if count % s == 0)
    per_step = count // steps
    unroll = next(s for s in (8, 6, 4, 3, 2, 1) if per_step % s == 0)
    shape = (leaves, x.shape[0], width)

    def kernel(*refs):
        local_kernel(unroll, *refs)

    return pl.pallas_call(
        kernel,
        grid=(steps,),
        out_shape=jax.ShapeDtypeStruct(shape, F32),
        in_specs=[
            smem(),
            vmem(),
            pl.BlockSpec((per_step, width, width), lambda i: (i, 0, 0)),
        ],
        out_specs=vmem(),
        scratch_shapes=[pltpu.VMEM(shape, F32)] * 4,
        compiler_params=params(),
        cost_estimate=pl.CostEstimate(
            flops=count * 4 * 32 * width * width * 16,
            bytes_accessed=blocks.size * 2,
            transcendentals=0,
        ),
        name="local_blocks",
    )(pairs.reshape(-1), x, blocks)


def far_kernel(neigh, cap, slots_ref, back_ref, mine_ref, far_ref, *refs):
    peers, got = refs[:neigh], refs[neigh : 2 * neigh]
    ahead_ref, behind_ref = refs[2 * neigh :]
    for k in range(neigh):
        for c in range(cap):
            place = (k * cap + c) * 2
            target = jnp.maximum(slots_ref[place], 0)
            source = jnp.maximum(slots_ref[place + 1], 0)
            lifted = mm(far_ref[k, c], mine_ref[target], TN).astype(BF16)
            ahead_ref[k, c] = mm(peers[k][source], lifted, TN).astype(BF16)
            target = jnp.maximum(back_ref[place], 0)
            source = jnp.maximum(back_ref[place + 1], 0)
            lifted = mm(got[k][c], mine_ref[source]).astype(BF16)
            behind_ref[k, c] = mm(peers[k][target], lifted, TN).astype(BF16)


def far_call(slots, back, bases, blocks, peer_bases, peer_blocks):
    neigh, cap = blocks.shape[0], blocks.shape[1]
    width = bases.shape[2]
    shape = jax.ShapeDtypeStruct((neigh, cap, width, width), BF16)

    def kernel(*refs):
        far_kernel(neigh, cap, *refs)

    return pl.pallas_call(
        kernel,
        out_shape=(shape, shape),
        in_specs=[smem(), smem()] + [vmem()] * (2 + 2 * neigh),
        out_specs=(vmem(), vmem()),
        compiler_params=params(),
        cost_estimate=pl.CostEstimate(flops=10**8, bytes_accessed=4 * 10**6, transcendentals=0),
        name="far_blocks",
    )(slots, back, bases, blocks, *peer_bases, *peer_blocks)


def join_kernel(
    neigh, near_ref, nback_ref, far_ref, fback_ref, local_ref, v_ref, w_ref, u_ref,
    blocks_ref, ahead_ref, behind_ref, *refs
):
    fields, got = refs[:neigh], refs[neigh : 2 * neigh]
    out_ref, next_ref, acc_a, acc_b = refs[2 * neigh :]
    leaves, rows, width = local_ref.shape
    acc_a[:leaves] = local_ref[...]
    acc_b[...] = jnp.zeros_like(acc_b)
    near_cap, far_cap = blocks_ref.shape[1], ahead_ref.shape[1]

    def parent(e, total):
        return total + mm(u_ref[e], w_ref[e])

    total = lax.fori_loop(0, u_ref.shape[0], parent, jnp.zeros(next_ref.shape, F32))
    down = total.astype(BF16)

    for k in range(neigh):
        work = []
        for c in range(near_cap + far_cap):
            if c < near_cap:
                go, back, place = near_ref, nback_ref, (k * near_cap + c) * 2
                ahead, behind, dims = blocks_ref[k, c], got[k][c], NT
            else:
                go, back, place = far_ref, fback_ref, (k * far_cap + c - near_cap) * 2
                ahead, behind, dims = ahead_ref[k, c - near_cap], behind_ref[k, c - near_cap], NN
            target, source = go[place], go[place + 1]
            there, here = back[place], back[place + 1]
            work.append(
                (
                    jnp.where(target < 0, leaves, target),
                    jnp.where(here < 0, leaves, here),
                    mm(leaf_cols(fields[k], jnp.maximum(source, 0), width), ahead),
                    mm(leaf_cols(fields[k], jnp.maximum(there, 0), width), behind, dims),
                )
            )
        for target, here, one, two in work:
            acc_a[target] += one
            acc_b[here] += two
    for leaf in range(leaves):
        cols = slice(leaf * width, (leaf + 1) * width)
        out_ref[:, cols] = (acc_a[leaf] + acc_b[leaf] + mm(down, v_ref[:, cols])).astype(BF16)
    next_ref[...] = mm(out_ref[...], v_ref[...], NT).astype(BF16)


def join_call(tables, local_sum, v, w, u_all, blocks, far, fields, got):
    neigh = blocks.shape[0]
    leaves, rows, width = local_sum.shape

    def kernel(*refs):
        join_kernel(neigh, *refs)

    return pl.pallas_call(
        kernel,
        out_shape=(
            jax.ShapeDtypeStruct((rows, leaves * width), BF16),
            jax.ShapeDtypeStruct((rows, v.shape[0]), BF16),
        ),
        in_specs=[smem()] * 4 + [vmem()] * (7 + 2 * neigh),
        out_specs=(vmem(), vmem()),
        scratch_shapes=[pltpu.VMEM((leaves + 1, rows, width), F32)] * 2,
        compiler_params=params(),
        cost_estimate=pl.CostEstimate(flops=10**9, bytes_accessed=8 * 10**6, transcendentals=0),
        name="near_and_join",
    )(*tables, local_sum, v, w, u_all, blocks, *far, *fields, *got)


def body(
    rhs,
    bases,
    transfers,
    near_slots,
    near_blocks,
    local_pairs,
    local_blocks,
    far_slots,
    far_blocks,
    parent_pairs,
    parent_blocks,
):
    neigh = near_slots.shape[1]
    offsets = neighbour_offsets(neigh)
    near, far = near_blocks[0], far_blocks[0]
    near_cap, far_cap = near.shape[1], far.shape[1]

    def send(pick):
        return [shifted(pick(neigh - 1 - k), "leaf", -offsets[k]) for k in range(neigh)]

    fields = send(lambda k: rhs)
    slots = jnp.concatenate([near_slots[0], far_slots[0]], axis=1)
    back = jnp.stack(send(lambda k: slots[k]))
    got_bases = send(lambda k: bases)
    got_far = send(lambda k: far[k])
    got_near = send(lambda k: near[k])
    tables = [
        near_slots.reshape(-1),
        back[:, :near_cap].reshape(-1),
        far_slots.reshape(-1),
        back[:, near_cap:].reshape(-1),
    ]

    v, u = start_call(rhs, bases, transfers)

    owners = lax.axis_size("leaf")
    me = lax.axis_index("leaf")
    all_blocks = lax.all_gather(parent_blocks[0], "leaf", axis=0)
    all_pairs = lax.all_gather(parent_pairs[0], "leaf", axis=0)
    ids = jnp.arange(owners, dtype=jnp.int32)
    mine = (parent_pairs[0][:, None] == ids[None, :]).astype(F32)
    theirs = (all_pairs == me).astype(F32)
    w = jnp.sum(
        mine[:, :, None, None] * parent_blocks[0].astype(F32).transpose(0, 2, 1)[:, None], axis=0
    ) + jnp.sum(theirs[:, :, None, None] * all_blocks.astype(F32), axis=1)
    w = w.astype(BF16)

    u_all = lax.all_gather(u, "leaf", axis=0)
    local_sum = local_call(rhs, local_pairs[0], local_blocks[0])
    effective = far_call(tables[2], tables[3], bases, far, got_bases, got_far)
    first, u = join_call(tables, local_sum, v, w, u_all, near, effective, fields, got_near)

    fields = send(lambda k: first)
    u_all = lax.all_gather(u, "leaf", axis=0)
    local_sum = local_call(first, local_pairs[0], local_blocks[0])
    second, _ = join_call(tables, local_sum, v, w, u_all, near, effective, fields, got_near)
    return (first, second)


def solution(mesh):
    in_specs = (
        P("groups", "leaf"),
        P(("groups", "leaf"), None, None),
        P(("groups", "leaf"), None, None),
        P(("groups", "leaf"), None, None, None),
        P(("groups", "leaf"), None, None, None, None),
        P(("groups", "leaf"), None, None),
        P(("groups", "leaf"), None, None, None),
        P(("groups", "leaf"), None, None, None),
        P(("groups", "leaf"), None, None, None, None),
        P(("groups", "leaf"), None),
        P(("groups", "leaf"), None, None, None),
    )
    out_specs = (P("groups", "leaf"), P("groups", "leaf"))
    return jax.shard_map(body, mesh=mesh, in_specs=in_specs, out_specs=out_specs, check_vma=False)
```

```python
import jax
import jax.numpy as jnp
from jax import lax
from jax.experimental import pallas as pl
from jax.experimental.pallas import tpu as pltpu
from jax.sharding import PartitionSpec as P

F32 = jnp.float32
BF16 = jnp.bfloat16
NN = (((1,), (0,)), ((), ()))
NT = (((1,), (1,)), ((), ()))
TN = (((0,), (0,)), ((), ()))


def mm(a, b, dims=NN):
    return lax.dot_general(a, b, dims, preferred_element_type=F32)


def neighbour_offsets(count):
    half = count // 2
    return [step - half if step < half else step - half + 1 for step in range(count)]


def vmem():
    return pl.BlockSpec(memory_space=pltpu.VMEM)


def smem():
    return pl.BlockSpec(memory_space=pltpu.SMEM)


def leaf_cols(ref, leaf, width):
    return ref[:, pl.ds(pl.multiple_of(leaf * width, width), width)]


def params():
    return pltpu.CompilerParams(vmem_limit_bytes=40 * 1024 * 1024)


def exchange_kernel(owners, offsets, whole, split, filled, *refs):
    neigh, count = len(offsets), whole + split
    sources, spread = refs[:count], refs[count]
    landed, gathered = refs[count + 1 : 2 * count + 1], refs[2 * count + 1]
    send, recv, spread_send, spread_recv, own = refs[2 * count + 2 :]
    me = lax.axis_index("leaf")
    barrier = pltpu.get_barrier_semaphore()

    def greet(i, carry):
        peer = lax.rem(me + i, owners)
        pl.semaphore_signal(
            barrier, inc=1, device_id={"leaf": peer}, device_id_type=pl.DeviceIdType.MESH
        )
        return carry

    lax.fori_loop(1, owners, greet, 0)

    def present(k):
        return (me + offsets[k] >= 0) & (me + offsets[k] < owners)

    if filled is not None:
        for k in range(neigh):

            @pl.when(jnp.logical_not(present(k)))
            def _():
                landed[filled][k] = jnp.full_like(landed[filled].at[k], -1)

    mine = pltpu.make_async_copy(spread_of(spread, me), gathered.at[me], own)
    mine.start()
    pl.semaphore_wait(barrier, owners - 1)

    def spread_copy(i):
        peer = lax.rem(me + i, owners)
        return pltpu.make_async_remote_copy(
            src_ref=spread_of(spread, peer),
            dst_ref=gathered.at[me],
            send_sem=spread_send.at[i],
            recv_sem=spread_recv.at[i],
            device_id={"leaf": peer},
            device_id_type=pl.DeviceIdType.MESH,
        )

    def spread_arrival(i):
        sender = lax.rem(me + owners - i, owners)
        return pltpu.make_async_remote_copy(
            src_ref=spread_of(spread, sender),
            dst_ref=gathered.at[sender],
            send_sem=spread_send.at[i],
            recv_sem=spread_recv.at[i],
            device_id={"leaf": sender},
            device_id_type=pl.DeviceIdType.MESH,
        )

    def copy(item, k, slot):
        source = sources[item] if item < whole else sources[item].at[k]
        return pltpu.make_async_remote_copy(
            src_ref=source,
            dst_ref=landed[item].at[slot],
            send_sem=send.at[item, k],
            recv_sem=recv.at[item, slot],
            device_id={"leaf": me + offsets[k]},
            device_id_type=pl.DeviceIdType.MESH,
        )

    for k in range(neigh):

        @pl.when(present(k))
        def _():
            for item in range(count):
                copy(item, k, neigh - 1 - k).start()

    def begin(i, carry):
        spread_copy(i).start()
        return carry

    def finish(i, carry):
        spread_copy(i).wait_send()
        spread_arrival(i).wait_recv()
        return carry

    lax.fori_loop(1, owners, begin, 0)
    mine.wait()
    lax.fori_loop(1, owners, finish, 0)
    for k in range(neigh):

        @pl.when(present(k))
        def _():
            for item in range(count):
                copy(item, k, k).wait_send()
                copy(item, k, k).wait_recv()


def spread_of(ref, owner):
    return ref.at[owner] if len(ref.shape) == 3 else ref


def exchange_call(ident, owners, offsets, whole, split, spread, filled=None):
    neigh = len(offsets)
    any_space = pl.BlockSpec(memory_space=pl.ANY)
    specs = [any_space] * (len(whole) + len(split))
    if filled is not None:
        specs[filled] = vmem()
    shapes = [jax.ShapeDtypeStruct((neigh,) + a.shape, a.dtype) for a in whole]
    shapes += [jax.ShapeDtypeStruct(a.shape, a.dtype) for a in split]
    shapes += [jax.ShapeDtypeStruct((owners,) + spread.shape[-2:], spread.dtype)]

    def kernel(*refs):
        exchange_kernel(owners, offsets, len(whole), len(split), filled, *refs)

    items = (len(whole) + len(split), neigh)
    return pl.pallas_call(
        kernel,
        out_shape=tuple(shapes),
        in_specs=specs + [any_space],
        out_specs=tuple(specs + [any_space]),
        scratch_shapes=[
            pltpu.SemaphoreType.DMA(items),
            pltpu.SemaphoreType.DMA(items),
            pltpu.SemaphoreType.DMA((owners,)),
            pltpu.SemaphoreType.DMA((owners,)),
            pltpu.SemaphoreType.DMA,
        ],
        compiler_params=pltpu.CompilerParams(
            collective_id=ident, has_side_effects=True, vmem_limit_bytes=40 * 1024 * 1024
        ),
        cost_estimate=pl.CostEstimate(flops=0, bytes_accessed=4 * 10**6, transcendentals=0),
        name="exchange",
    )(*whole, *split, spread)


def start_kernel(x_ref, bases_ref, transfers_ref, v_ref, u_ref):
    leaves, _, width = bases_ref.shape
    for leaf in range(leaves):
        v_ref[:, leaf * width : (leaf + 1) * width] = mm(
            transfers_ref[leaf], bases_ref[leaf]
        ).astype(BF16)
    u_ref[...] = mm(x_ref[...], v_ref[...], NT).astype(BF16)


def start_call(x, bases, transfers):
    rank = bases.shape[1]
    return pl.pallas_call(
        start_kernel,
        out_shape=(
            jax.ShapeDtypeStruct((rank, x.shape[1]), BF16),
            jax.ShapeDtypeStruct((x.shape[0], rank), BF16),
        ),
        in_specs=[vmem()] * 3,
        out_specs=(vmem(), vmem()),
        compiler_params=params(),
        cost_estimate=pl.CostEstimate(flops=10**7, bytes_accessed=10**6, transcendentals=0),
        name="parent_basis",
    )(x, bases, transfers)


def local_kernel(unroll, pairs_ref, x_ref, blocks_ref, out_ref, *accs):
    step = pl.program_id(0)
    per_step, width = blocks_ref.shape[0], blocks_ref.shape[1]

    @pl.when(step == 0)
    def _():
        for acc in accs:
            acc[...] = jnp.zeros_like(acc)

    def group(i, carry):
        base = i * unroll
        work = []
        for j in range(unroll):
            place = (step * per_step + base + j) * 2
            target, source = pairs_ref[place], pairs_ref[place + 1]
            block = blocks_ref[base + j]
            work.append(
                (
                    target,
                    source,
                    mm(leaf_cols(x_ref, source, width), block),
                    mm(leaf_cols(x_ref, target, width), block, NT),
                )
            )
        for j, (target, source, to_target, to_source) in enumerate(work):
            first, second = accs[2 * (j % 2)], accs[2 * (j % 2) + 1]
            first[target] += to_target
            second[source] += to_source
        return carry

    lax.fori_loop(0, per_step // unroll, group, 0)

    @pl.when(step == pl.num_programs(0) - 1)
    def _():
        out_ref[...] = (accs[0][...] + accs[1][...]) + (accs[2][...] + accs[3][...])


def local_call(x, pairs, blocks):
    count, width = blocks.shape[0], blocks.shape[1]
    leaves = x.shape[1] // width
    steps = next(s for s in (6, 4, 3, 2, 1) if count % s == 0)
    per_step = count // steps
    unroll = next(s for s in (8, 6, 4, 3, 2, 1) if per_step % s == 0)
    shape = (leaves, x.shape[0], width)

    def kernel(*refs):
        local_kernel(unroll, *refs)

    return pl.pallas_call(
        kernel,
        grid=(steps,),
        out_shape=jax.ShapeDtypeStruct(shape, F32),
        in_specs=[
            smem(),
            vmem(),
            pl.BlockSpec((per_step, width, width), lambda i: (i, 0, 0)),
        ],
        out_specs=vmem(),
        scratch_shapes=[pltpu.VMEM(shape, F32)] * 4,
        compiler_params=params(),
        cost_estimate=pl.CostEstimate(
            flops=count * 4 * 32 * width * width * 16,
            bytes_accessed=blocks.size * 2,
            transcendentals=0,
        ),
        name="local_blocks",
    )(pairs.reshape(-1), x, blocks)


def far_kernel(neigh, cap, slots_ref, back_ref, mine_ref, far_ref, *refs):
    peers, got, ahead_ref, behind_ref = refs
    for k in range(neigh):
        for c in range(cap):
            place = (k * cap + c) * 2
            target = jnp.maximum(slots_ref[place], 0)
            source = jnp.maximum(slots_ref[place + 1], 0)
            lifted = mm(far_ref[k, c], mine_ref[target], TN).astype(BF16)
            ahead_ref[k, c] = mm(peers[k, source], lifted, TN).astype(BF16)
            target = jnp.maximum(back_ref[place], 0)
            source = jnp.maximum(back_ref[place + 1], 0)
            lifted = mm(got[k, c], mine_ref[source]).astype(BF16)
            behind_ref[k, c] = mm(peers[k, target], lifted, TN).astype(BF16)


def far_call(slots, back, bases, blocks, peer_bases, peer_blocks):
    neigh, cap = blocks.shape[0], blocks.shape[1]
    width = bases.shape[2]
    shape = jax.ShapeDtypeStruct((neigh, cap, width, width), BF16)

    def kernel(*refs):
        far_kernel(neigh, cap, *refs)

    return pl.pallas_call(
        kernel,
        out_shape=(shape, shape),
        in_specs=[smem(), smem()] + [vmem()] * 4,
        out_specs=(vmem(), vmem()),
        compiler_params=params(),
        cost_estimate=pl.CostEstimate(flops=10**8, bytes_accessed=4 * 10**6, transcendentals=0),
        name="far_blocks",
    )(slots, back, bases, blocks, peer_bases, peer_blocks)


def join_kernel(
    neigh, near_ref, nback_ref, far_ref, fback_ref, local_ref, v_ref, w_ref, u_ref,
    blocks_ref, ahead_ref, behind_ref, *refs
):
    fields, got, out_ref, next_ref, acc_a, acc_b = refs
    rank = v_ref.shape[0]
    leaves, rows, width = local_ref.shape
    acc_a[:leaves] = local_ref[...]
    acc_b[...] = jnp.zeros_like(acc_b)
    near_cap, far_cap = blocks_ref.shape[1], ahead_ref.shape[1]

    def parent(e, total):
        return total + mm(u_ref[e][:, :rank], w_ref[e])

    total = lax.fori_loop(0, u_ref.shape[0], parent, jnp.zeros((rows, rank), F32))
    down = total.astype(BF16)

    for k in range(neigh):
        work = []
        for c in range(near_cap + far_cap):
            if c < near_cap:
                go, back, place = near_ref, nback_ref, (k * near_cap + c) * 2
                ahead, behind, dims = blocks_ref[k, c], got[k, c], NT
            else:
                go, back, place = far_ref, fback_ref, (k * far_cap + c - near_cap) * 2
                ahead, behind, dims = ahead_ref[k, c - near_cap], behind_ref[k, c - near_cap], NN
            target, source = go[place], go[place + 1]
            there, here = back[place], back[place + 1]
            work.append(
                (
                    jnp.where(target < 0, leaves, target),
                    jnp.where(here < 0, leaves, here),
                    mm(leaf_cols(fields.at[k], jnp.maximum(source, 0), width), ahead),
                    mm(leaf_cols(fields.at[k], jnp.maximum(there, 0), width), behind, dims),
                )
            )
        for target, here, one, two in work:
            acc_a[target] += one
            acc_b[here] += two
    for leaf in range(leaves):
        cols = slice(leaf * width, (leaf + 1) * width)
        out_ref[:, cols] = (acc_a[leaf] + acc_b[leaf] + mm(down, v_ref[:, cols])).astype(BF16)
    next_ref[...] = jnp.zeros_like(next_ref)
    next_ref[:, :rank] = mm(out_ref[...], v_ref[...], NT).astype(BF16)


def join_call(tables, local_sum, v, w, u_all, blocks, far, fields, got):
    neigh = blocks.shape[0]
    leaves, rows, width = local_sum.shape

    def kernel(*refs):
        join_kernel(neigh, *refs)

    return pl.pallas_call(
        kernel,
        out_shape=(
            jax.ShapeDtypeStruct((rows, leaves * width), BF16),
            jax.ShapeDtypeStruct((rows, width), BF16),
        ),
        in_specs=[smem()] * 4 + [vmem()] * 9,
        out_specs=(vmem(), vmem()),
        scratch_shapes=[pltpu.VMEM((leaves + 1, rows, width), F32)] * 2,
        compiler_params=params(),
        cost_estimate=pl.CostEstimate(flops=10**9, bytes_accessed=8 * 10**6, transcendentals=0),
        name="near_and_join",
    )(*tables, local_sum, v, w, u_all, blocks, *far, fields, got)


def exchange_first(owners, offsets, flat, rhs, bases, near, far, spread):
    fields, got_bases, flat_got, got_near, got_far, u_all = exchange_call(
        0, owners, offsets, [rhs, bases], [flat, near, far], spread, filled=2
    )
    return flat_got, fields, got_bases, got_near, got_far, u_all


def body(
    rhs,
    bases,
    transfers,
    near_slots,
    near_blocks,
    local_pairs,
    local_blocks,
    far_slots,
    far_blocks,
    parent_pairs,
    parent_blocks,
):
    neigh = near_slots.shape[1]
    offsets = neighbour_offsets(neigh)
    near, far = near_blocks[0], far_blocks[0]
    near_cap, far_cap = near.shape[1], far.shape[1]

    owners = lax.axis_size("leaf")
    lanes = bases.shape[2]
    slots = jnp.concatenate([near_slots[0], far_slots[0]], axis=1)
    flat = slots.reshape(neigh, 1, -1)
    flat = jnp.pad(flat, ((0, 0), (0, 7), (0, lanes - flat.shape[2])))

    v, u = start_call(rhs, bases, transfers)

    ids = jnp.arange(owners, dtype=jnp.int32)
    live = (parent_pairs[0][:, None] == ids[None, :]).astype(F32)[:, :, None, None]
    parents = parent_blocks[0].astype(F32)
    returned = jnp.sum(live * parents[:, None], axis=0).astype(BF16)
    rank = returned.shape[1]
    spread = jnp.concatenate(
        [
            jnp.broadcast_to(u[None], (owners,) + u.shape),
            returned,
            jnp.zeros((owners, rank, lanes - 2 * rank), BF16),
        ],
        axis=2,
    )
    flat_got, fields, got_bases, got_near, got_far, u_all = exchange_first(
        owners, offsets, flat, rhs, bases, near, far, spread
    )
    back = flat_got[:, 0, : 2 * (near_cap + far_cap)].reshape(neigh, near_cap + far_cap, 2)
    tables = [
        near_slots.reshape(-1),
        back[:, :near_cap].reshape(-1),
        far_slots.reshape(-1),
        back[:, near_cap:].reshape(-1),
    ]
    w = jnp.sum(live * parents.transpose(0, 2, 1)[:, None], axis=0)
    w = (w + u_all[:, :, rank : 2 * rank].astype(F32)).astype(BF16)

    local_sum = local_call(rhs, local_pairs[0], local_blocks[0])
    effective = far_call(tables[2], tables[3], bases, far, got_bases, got_far)
    first, u = join_call(tables, local_sum, v, w, u_all, near, effective, fields, got_near)

    fields, u_all = exchange_call(1, owners, offsets, [first], [], u)
    local_sum = local_call(first, local_pairs[0], local_blocks[0])
    second, _ = join_call(tables, local_sum, v, w, u_all, near, effective, fields, got_near)
    return (first, second)


def solution(mesh):
    in_specs = (
        P("groups", "leaf"),
        P(("groups", "leaf"), None, None),
        P(("groups", "leaf"), None, None),
        P(("groups", "leaf"), None, None, None),
        P(("groups", "leaf"), None, None, None, None),
        P(("groups", "leaf"), None, None),
        P(("groups", "leaf"), None, None, None),
        P(("groups", "leaf"), None, None, None),
        P(("groups", "leaf"), None, None, None, None),
        P(("groups", "leaf"), None),
        P(("groups", "leaf"), None, None, None),
    )
    out_specs = (P("groups", "leaf"), P("groups", "leaf"))
    return jax.shard_map(body, mesh=mesh, in_specs=in_specs, out_specs=out_specs, check_vma=False)
```

```python
import jax
import jax.numpy as jnp
from jax import lax
from jax.experimental import pallas as pl
from jax.experimental.pallas import tpu as pltpu
from jax.sharding import PartitionSpec as P

F32 = jnp.float32
BF16 = jnp.bfloat16
NN = (((1,), (0,)), ((), ()))
NT = (((1,), (1,)), ((), ()))
TN = (((0,), (0,)), ((), ()))


def mm(a, b, dims=NN):
    return lax.dot_general(a, b, dims, preferred_element_type=F32)


def neighbour_offsets(count):
    half = count // 2
    return [step - half if step < half else step - half + 1 for step in range(count)]


def vmem():
    return pl.BlockSpec(memory_space=pltpu.VMEM)


def smem():
    return pl.BlockSpec(memory_space=pltpu.SMEM)


def leaf_cols(ref, leaf, width):
    return ref[:, pl.ds(pl.multiple_of(leaf * width, width), width)]


def params():
    return pltpu.CompilerParams(vmem_limit_bytes=60 * 1024 * 1024)


def exchange_kernel(owners, offsets, whole, split, filled, *refs):
    neigh, count = len(offsets), whole + split
    sources, spread = refs[:count], refs[count]
    landed, gathered = refs[count + 1 : 2 * count + 1], refs[2 * count + 1]
    send, recv, spread_send, spread_recv, own, onward = refs[2 * count + 2 :]
    me = lax.axis_index("leaf")
    barrier = pltpu.get_barrier_semaphore()

    def greet(i, carry):
        peer = lax.rem(me + i, owners)
        pl.semaphore_signal(
            barrier, inc=1, device_id={"leaf": peer}, device_id_type=pl.DeviceIdType.MESH
        )
        return carry

    lax.fori_loop(1, owners, greet, 0)

    def present(k):
        return (me + offsets[k] >= 0) & (me + offsets[k] < owners)

    if filled is not None:
        for k in range(neigh):

            @pl.when(jnp.logical_not(present(k)))
            def _():
                landed[filled][k] = jnp.full_like(landed[filled].at[k], -1)

    mine = pltpu.make_async_copy(spread_of(spread, me), gathered.at[me], own)
    mine.start()
    pl.semaphore_wait(barrier, owners - 1)

    def spread_copy(i):
        peer = lax.rem(me + i, owners)
        return pltpu.make_async_remote_copy(
            src_ref=spread_of(spread, peer),
            dst_ref=gathered.at[me],
            send_sem=spread_send.at[i],
            recv_sem=spread_recv.at[i],
            device_id={"leaf": peer},
            device_id_type=pl.DeviceIdType.MESH,
        )

    def spread_arrival(i):
        sender = lax.rem(me + owners - i, owners)
        return pltpu.make_async_remote_copy(
            src_ref=spread_of(spread, sender),
            dst_ref=gathered.at[sender],
            send_sem=spread_send.at[i],
            recv_sem=spread_recv.at[i],
            device_id={"leaf": sender},
            device_id_type=pl.DeviceIdType.MESH,
        )

    def copy(item, k, slot):
        source = sources[item] if item < whole else sources[item].at[k]
        return pltpu.make_async_remote_copy(
            src_ref=source,
            dst_ref=landed[item].at[slot],
            send_sem=send.at[item, k],
            recv_sem=recv.at[item, slot],
            device_id={"leaf": me + offsets[k]},
            device_id_type=pl.DeviceIdType.MESH,
        )

    parity = lax.rem(me, 2)

    def direct(k):
        step = offsets[k]
        if step % 2 == 0:
            return present(k)
        relayed = [step - 1 in offsets, step + 1 in offsets]
        return present(k) & ((parity == 0) & (not relayed[0]) | (parity == 1) & (not relayed[1]))

    def relay(item, k, side):
        slot = offsets.index(offsets[k] + (1 if side else -1))
        return pltpu.make_async_remote_copy(
            src_ref=landed[item].at[k],
            dst_ref=landed[item].at[slot],
            send_sem=onward.at[item, k],
            recv_sem=recv.at[item, slot],
            device_id={"leaf": me + (-1 if side else 1)},
            device_id_type=pl.DeviceIdType.MESH,
        )

    relays = [
        (k, side)
        for k in range(neigh)
        for side in (0, 1)
        if offsets[k] % 2 == 0 and offsets[k] + (1 if side else -1) in offsets
    ]

    for k in range(neigh):

        @pl.when(direct(k))
        def _():
            for item in range(whole):
                copy(item, k, neigh - 1 - k).start()

    for k in range(neigh):

        @pl.when(present(k))
        def _():
            for item in range(whole, count):
                copy(item, k, neigh - 1 - k).start()

    def begin(i, carry):
        spread_copy(i).start()
        return carry

    def finish(i, carry):
        spread_copy(i).wait_send()
        spread_arrival(i).wait_recv()
        return carry

    lax.fori_loop(1, owners, begin, 0)
    mine.wait()
    lax.fori_loop(1, owners, finish, 0)
    for k in range(neigh):
        if offsets[k] % 2 == 0:

            @pl.when(present(k))
            def _():
                for item in range(whole):
                    copy(item, k, k).wait_recv()

            for place, side in relays:
                if place == k:

                    @pl.when(present(k) & (parity == side))
                    def _():
                        for item in range(whole):
                            relay(item, k, side).start()

    for k in range(neigh):

        @pl.when(direct(k))
        def _():
            for item in range(whole):
                copy(item, k, k).wait_send()

        @pl.when(present(k))
        def _():
            for item in range(whole if offsets[k] % 2 == 0 else 0, count):
                copy(item, k, k).wait_recv()
            for item in range(whole, count):
                copy(item, k, k).wait_send()

    for k, side in relays:

        @pl.when(present(k) & (parity == side))
        def _():
            for item in range(whole):
                relay(item, k, side).wait_send()


def spread_of(ref, owner):
    return ref.at[owner] if len(ref.shape) == 3 else ref


def exchange_call(ident, owners, offsets, whole, split, spread, filled=None):
    neigh = len(offsets)
    any_space = pl.BlockSpec(memory_space=pl.ANY)
    specs = [any_space] * (len(whole) + len(split))
    if filled is not None:
        specs[filled] = vmem()
    shapes = [jax.ShapeDtypeStruct((neigh,) + a.shape, a.dtype) for a in whole]
    shapes += [jax.ShapeDtypeStruct(a.shape, a.dtype) for a in split]
    shapes += [jax.ShapeDtypeStruct((owners,) + spread.shape[-2:], spread.dtype)]

    def kernel(*refs):
        exchange_kernel(owners, offsets, len(whole), len(split), filled, *refs)

    items = (len(whole) + len(split), neigh)
    return pl.pallas_call(
        kernel,
        out_shape=tuple(shapes),
        in_specs=specs + [any_space],
        out_specs=tuple(specs + [any_space]),
        scratch_shapes=[
            pltpu.SemaphoreType.DMA(items),
            pltpu.SemaphoreType.DMA(items),
            pltpu.SemaphoreType.DMA((owners,)),
            pltpu.SemaphoreType.DMA((owners,)),
            pltpu.SemaphoreType.DMA,
            pltpu.SemaphoreType.DMA(items),
        ],
        compiler_params=pltpu.CompilerParams(
            collective_id=ident, has_side_effects=True, vmem_limit_bytes=40 * 1024 * 1024
        ),
        cost_estimate=pl.CostEstimate(flops=0, bytes_accessed=4 * 10**6, transcendentals=0),
        name="exchange",
    )(*whole, *split, spread)


def start_kernel(x_ref, bases_ref, transfers_ref, v_ref, u_ref):
    leaves, _, width = bases_ref.shape
    for leaf in range(leaves):
        v_ref[:, leaf * width : (leaf + 1) * width] = mm(
            transfers_ref[leaf], bases_ref[leaf]
        ).astype(BF16)
    u_ref[...] = mm(x_ref[...], v_ref[...], NT).astype(BF16)


def start_call(x, bases, transfers):
    rank = bases.shape[1]
    return pl.pallas_call(
        start_kernel,
        out_shape=(
            jax.ShapeDtypeStruct((rank, x.shape[1]), BF16),
            jax.ShapeDtypeStruct((x.shape[0], rank), BF16),
        ),
        in_specs=[vmem()] * 3,
        out_specs=(vmem(), vmem()),
        compiler_params=params(),
        cost_estimate=pl.CostEstimate(flops=10**7, bytes_accessed=10**6, transcendentals=0),
        name="parent_basis",
    )(x, bases, transfers)


def local_kernel(unroll, pairs_ref, x_ref, blocks_ref, out_ref, *accs):
    step = pl.program_id(0)
    per_step, width = blocks_ref.shape[0], blocks_ref.shape[1]

    @pl.when(step == 0)
    def _():
        for acc in accs:
            acc[...] = jnp.zeros_like(acc)

    def group(i, carry):
        base = i * unroll
        work = []
        for j in range(unroll):
            place = (step * per_step + base + j) * 2
            target, source = pairs_ref[place], pairs_ref[place + 1]
            block = blocks_ref[base + j]
            work.append(
                (
                    target,
                    source,
                    mm(leaf_cols(x_ref, source, width), block),
                    mm(leaf_cols(x_ref, target, width), block, NT),
                )
            )
        for j, (target, source, to_target, to_source) in enumerate(work):
            first, second = accs[2 * (j % 2)], accs[2 * (j % 2) + 1]
            first[target] += to_target
            second[source] += to_source
        return carry

    lax.fori_loop(0, per_step // unroll, group, 0)

    @pl.when(step == pl.num_programs(0) - 1)
    def _():
        out_ref[...] = (accs[0][...] + accs[1][...]) + (accs[2][...] + accs[3][...])


def local_call(x, pairs, blocks):
    count, width = blocks.shape[0], blocks.shape[1]
    leaves = x.shape[1] // width
    steps = next(s for s in (6, 4, 3, 2, 1) if count % s == 0)
    per_step = count // steps
    unroll = next(s for s in (8, 6, 4, 3, 2, 1) if per_step % s == 0)
    shape = (leaves, x.shape[0], width)

    def kernel(*refs):
        local_kernel(unroll, *refs)

    return pl.pallas_call(
        kernel,
        grid=(steps,),
        out_shape=jax.ShapeDtypeStruct(shape, F32),
        in_specs=[
            smem(),
            vmem(),
            pl.BlockSpec((per_step, width, width), lambda i: (i, 0, 0)),
        ],
        out_specs=vmem(),
        scratch_shapes=[pltpu.VMEM(shape, F32)] * 4,
        compiler_params=params(),
        cost_estimate=pl.CostEstimate(
            flops=count * 4 * 32 * width * width * 16,
            bytes_accessed=blocks.size * 2,
            transcendentals=0,
        ),
        name="local_blocks",
    )(pairs.reshape(-1), x, blocks)


def far_kernel(neigh, cap, slots_ref, back_ref, mine_ref, far_ref, *refs):
    peers, got, ahead_ref, behind_ref = refs
    for k in range(neigh):
        for c in range(cap):
            place = (k * cap + c) * 2
            target = jnp.maximum(slots_ref[place], 0)
            source = jnp.maximum(slots_ref[place + 1], 0)
            lifted = mm(far_ref[k, c], mine_ref[target], TN).astype(BF16)
            ahead_ref[k, c] = mm(peers[k, source], lifted, TN).astype(BF16)
            target = jnp.maximum(back_ref[place], 0)
            source = jnp.maximum(back_ref[place + 1], 0)
            lifted = mm(got[k, c], mine_ref[source]).astype(BF16)
            behind_ref[k, c] = mm(peers[k, target], lifted, TN).astype(BF16)


def far_call(slots, back, bases, blocks, peer_bases, peer_blocks):
    neigh, cap = blocks.shape[0], blocks.shape[1]
    width = bases.shape[2]
    shape = jax.ShapeDtypeStruct((neigh, cap, width, width), BF16)

    def kernel(*refs):
        far_kernel(neigh, cap, *refs)

    return pl.pallas_call(
        kernel,
        out_shape=(shape, shape),
        in_specs=[smem(), smem()] + [vmem()] * 4,
        out_specs=(vmem(), vmem()),
        compiler_params=params(),
        cost_estimate=pl.CostEstimate(flops=10**8, bytes_accessed=4 * 10**6, transcendentals=0),
        name="far_blocks",
    )(slots, back, bases, blocks, peer_bases, peer_blocks)


def join_kernel(
    neigh, near_ref, nback_ref, far_ref, fback_ref, local_ref, v_ref, w_ref, u_ref,
    blocks_ref, ahead_ref, behind_ref, *refs
):
    fields, got, out_ref, next_ref, acc_a, acc_b = refs
    rank = v_ref.shape[0]
    leaves, rows, width = local_ref.shape
    acc_a[:leaves] = local_ref[...]
    acc_b[...] = jnp.zeros_like(acc_b)
    near_cap, far_cap = blocks_ref.shape[1], ahead_ref.shape[1]

    def parent(e, total):
        return total + mm(u_ref[e][:, :rank], w_ref[e])

    total = lax.fori_loop(0, u_ref.shape[0], parent, jnp.zeros((rows, rank), F32))
    down = total.astype(BF16)

    for k in range(neigh):
        work = []
        for c in range(near_cap + far_cap):
            if c < near_cap:
                go, back, place = near_ref, nback_ref, (k * near_cap + c) * 2
                ahead, behind, dims = blocks_ref[k, c], got[k, c], NT
            else:
                go, back, place = far_ref, fback_ref, (k * far_cap + c - near_cap) * 2
                ahead, behind, dims = ahead_ref[k, c - near_cap], behind_ref[k, c - near_cap], NN
            target, source = go[place], go[place + 1]
            there, here = back[place], back[place + 1]
            work.append(
                (
                    jnp.where(target < 0, leaves, target),
                    jnp.where(here < 0, leaves, here),
                    mm(leaf_cols(fields.at[k], jnp.maximum(source, 0), width), ahead),
                    mm(leaf_cols(fields.at[k], jnp.maximum(there, 0), width), behind, dims),
                )
            )
        for target, here, one, two in work:
            acc_a[target] += one
            acc_b[here] += two
    for leaf in range(leaves):
        cols = slice(leaf * width, (leaf + 1) * width)
        out_ref[:, cols] = (acc_a[leaf] + acc_b[leaf] + mm(down, v_ref[:, cols])).astype(BF16)
    next_ref[...] = jnp.zeros_like(next_ref)
    next_ref[:, :rank] = mm(out_ref[...], v_ref[...], NT).astype(BF16)


def join_call(tables, local_sum, v, w, u_all, blocks, far, fields, got):
    neigh = blocks.shape[0]
    leaves, rows, width = local_sum.shape

    def kernel(*refs):
        join_kernel(neigh, *refs)

    return pl.pallas_call(
        kernel,
        out_shape=(
            jax.ShapeDtypeStruct((rows, leaves * width), BF16),
            jax.ShapeDtypeStruct((rows, width), BF16),
        ),
        in_specs=[smem()] * 4 + [vmem()] * 9,
        out_specs=(vmem(), vmem()),
        scratch_shapes=[pltpu.VMEM((leaves + 1, rows, width), F32)] * 2,
        compiler_params=params(),
        cost_estimate=pl.CostEstimate(flops=10**9, bytes_accessed=8 * 10**6, transcendentals=0),
        name="near_and_join",
    )(*tables, local_sum, v, w, u_all, blocks, *far, fields, got)


def exchange_first(owners, offsets, flat, rhs, bases, near, far, spread):
    fields, got_bases, flat_got, got_near, got_far, u_all = exchange_call(
        0, owners, offsets, [rhs, bases], [flat, near, far], spread, filled=2
    )
    return flat_got, fields, got_bases, got_near, got_far, u_all


def body(
    rhs,
    bases,
    transfers,
    near_slots,
    near_blocks,
    local_pairs,
    local_blocks,
    far_slots,
    far_blocks,
    parent_pairs,
    parent_blocks,
):
    neigh = near_slots.shape[1]
    offsets = neighbour_offsets(neigh)
    near, far = near_blocks[0], far_blocks[0]
    near_cap, far_cap = near.shape[1], far.shape[1]

    owners = lax.axis_size("leaf")
    lanes = bases.shape[2]
    slots = jnp.concatenate([near_slots[0], far_slots[0]], axis=1)
    flat = slots.reshape(neigh, 1, -1)
    flat = jnp.pad(flat, ((0, 0), (0, 7), (0, lanes - flat.shape[2])))

    v, u = start_call(rhs, bases, transfers)

    ids = jnp.arange(owners, dtype=jnp.int32)
    live = (parent_pairs[0][:, None] == ids[None, :]).astype(F32)[:, :, None, None]
    parents = parent_blocks[0].astype(F32)
    returned = jnp.sum(live * parents[:, None], axis=0).astype(BF16)
    rank = returned.shape[1]
    spread = jnp.concatenate(
        [
            jnp.broadcast_to(u[None], (owners,) + u.shape),
            returned,
            jnp.zeros((owners, rank, lanes - 2 * rank), BF16),
        ],
        axis=2,
    )
    flat_got, fields, got_bases, got_near, got_far, u_all = exchange_first(
        owners, offsets, flat, rhs, bases, near, far, spread
    )
    back = flat_got[:, 0, : 2 * (near_cap + far_cap)].reshape(neigh, near_cap + far_cap, 2)
    tables = [
        near_slots.reshape(-1),
        back[:, :near_cap].reshape(-1),
        far_slots.reshape(-1),
        back[:, near_cap:].reshape(-1),
    ]
    w = jnp.sum(live * parents.transpose(0, 2, 1)[:, None], axis=0)
    w = (w + u_all[:, :, rank : 2 * rank].astype(F32)).astype(BF16)

    local_sum = local_call(rhs, local_pairs[0], local_blocks[0])
    effective = far_call(tables[2], tables[3], bases, far, got_bases, got_far)
    first, u = join_call(tables, local_sum, v, w, u_all, near, effective, fields, got_near)

    fields, u_all = exchange_call(1, owners, offsets, [first], [], u)
    local_sum = local_call(first, local_pairs[0], local_blocks[0])
    second, _ = join_call(tables, local_sum, v, w, u_all, near, effective, fields, got_near)
    return (first, second)


def solution(mesh):
    in_specs = (
        P("groups", "leaf"),
        P(("groups", "leaf"), None, None),
        P(("groups", "leaf"), None, None),
        P(("groups", "leaf"), None, None, None),
        P(("groups", "leaf"), None, None, None, None),
        P(("groups", "leaf"), None, None),
        P(("groups", "leaf"), None, None, None),
        P(("groups", "leaf"), None, None, None),
        P(("groups", "leaf"), None, None, None, None),
        P(("groups", "leaf"), None),
        P(("groups", "leaf"), None, None, None),
    )
    out_specs = (P("groups", "leaf"), P("groups", "leaf"))
    return jax.shard_map(body, mesh=mesh, in_specs=in_specs, out_specs=out_specs, check_vma=False)
```

```python
import jax
import jax.numpy as jnp
from jax import lax
from jax.experimental import pallas as pl
from jax.experimental.pallas import tpu as pltpu
from jax.sharding import PartitionSpec as P

F32 = jnp.float32
BF16 = jnp.bfloat16
NN = (((1,), (0,)), ((), ()))
NT = (((1,), (1,)), ((), ()))
TN = (((0,), (0,)), ((), ()))


def mm(a, b, dims=NN):
    return lax.dot_general(a, b, dims, preferred_element_type=F32)


def neighbour_offsets(count):
    half = count // 2
    return [step - half if step < half else step - half + 1 for step in range(count)]


def vmem():
    return pl.BlockSpec(memory_space=pltpu.VMEM)


def smem():
    return pl.BlockSpec(memory_space=pltpu.SMEM)


def leaf_cols(ref, leaf, width):
    return ref[:, pl.ds(pl.multiple_of(leaf * width, width), width)]


def params():
    return pltpu.CompilerParams(vmem_limit_bytes=60 * 1024 * 1024)


def exchange_kernel(owners, offsets, whole, split, filled, *refs):
    neigh, count = len(offsets), whole + split
    sources, spread = refs[:count], refs[count]
    landed, gathered = refs[count + 1 : 2 * count + 1], refs[2 * count + 1]
    send, recv, spread_send, spread_recv, own, onward = refs[2 * count + 2 :]
    me = lax.axis_index("leaf")
    barrier = pltpu.get_barrier_semaphore()

    def greet(i, carry):
        peer = lax.rem(me + i, owners)
        pl.semaphore_signal(
            barrier, inc=1, device_id={"leaf": peer}, device_id_type=pl.DeviceIdType.MESH
        )
        return carry

    lax.fori_loop(1, owners, greet, 0)

    def present(k):
        return (me + offsets[k] >= 0) & (me + offsets[k] < owners)

    if filled is not None:
        for k in range(neigh):

            @pl.when(jnp.logical_not(present(k)))
            def _():
                landed[filled][k] = jnp.full_like(landed[filled].at[k], -1)

    mine = pltpu.make_async_copy(spread_of(spread, me), gathered.at[me], own)
    mine.start()
    pl.semaphore_wait(barrier, owners - 1)

    def spread_copy(i):
        peer = lax.rem(me + i, owners)
        return pltpu.make_async_remote_copy(
            src_ref=spread_of(spread, peer),
            dst_ref=gathered.at[me],
            send_sem=spread_send.at[i],
            recv_sem=spread_recv.at[i],
            device_id={"leaf": peer},
            device_id_type=pl.DeviceIdType.MESH,
        )

    def spread_arrival(i):
        sender = lax.rem(me + owners - i, owners)
        return pltpu.make_async_remote_copy(
            src_ref=spread_of(spread, sender),
            dst_ref=gathered.at[sender],
            send_sem=spread_send.at[i],
            recv_sem=spread_recv.at[i],
            device_id={"leaf": sender},
            device_id_type=pl.DeviceIdType.MESH,
        )

    def copy(item, k, slot):
        source = sources[item] if item < whole else sources[item].at[k]
        return pltpu.make_async_remote_copy(
            src_ref=source,
            dst_ref=landed[item].at[slot],
            send_sem=send.at[item, k],
            recv_sem=recv.at[item, slot],
            device_id={"leaf": me + offsets[k]},
            device_id_type=pl.DeviceIdType.MESH,
        )

    parity = lax.rem(me, 2)

    def direct(k):
        step = offsets[k]
        if step % 2 == 0:
            return present(k)
        relayed = [step - 1 in offsets, step + 1 in offsets]
        return present(k) & ((parity == 0) & (not relayed[0]) | (parity == 1) & (not relayed[1]))

    def relay(item, k, side):
        slot = offsets.index(offsets[k] + (1 if side else -1))
        return pltpu.make_async_remote_copy(
            src_ref=landed[item].at[k],
            dst_ref=landed[item].at[slot],
            send_sem=onward.at[item, k],
            recv_sem=recv.at[item, slot],
            device_id={"leaf": me + (-1 if side else 1)},
            device_id_type=pl.DeviceIdType.MESH,
        )

    relays = [
        (k, side)
        for k in range(neigh)
        for side in (0, 1)
        if offsets[k] % 2 == 0 and offsets[k] + (1 if side else -1) in offsets
    ]

    for k in range(neigh):

        @pl.when(direct(k))
        def _():
            for item in range(whole):
                copy(item, k, neigh - 1 - k).start()

    for k in range(neigh):

        @pl.when(present(k))
        def _():
            for item in range(whole, count):
                copy(item, k, neigh - 1 - k).start()

    def begin(i, carry):
        spread_copy(i).start()
        return carry

    def finish(i, carry):
        spread_copy(i).wait_send()
        spread_arrival(i).wait_recv()
        return carry

    lax.fori_loop(1, owners, begin, 0)
    mine.wait()
    lax.fori_loop(1, owners, finish, 0)
    for k in range(neigh):
        if offsets[k] % 2 == 0:

            @pl.when(present(k))
            def _():
                for item in range(whole):
                    copy(item, k, k).wait_recv()

            for place, side in relays:
                if place == k:

                    @pl.when(present(k) & (parity == side))
                    def _():
                        for item in range(whole):
                            relay(item, k, side).start()

    for k in range(neigh):

        @pl.when(direct(k))
        def _():
            for item in range(whole):
                copy(item, k, k).wait_send()

        @pl.when(present(k))
        def _():
            for item in range(whole if offsets[k] % 2 == 0 else 0, count):
                copy(item, k, k).wait_recv()
            for item in range(whole, count):
                copy(item, k, k).wait_send()

    for k, side in relays:

        @pl.when(present(k) & (parity == side))
        def _():
            for item in range(whole):
                relay(item, k, side).wait_send()


def spread_of(ref, owner):
    return ref.at[owner] if len(ref.shape) == 3 else ref


def exchange_call(ident, owners, offsets, whole, split, spread, filled=None):
    neigh = len(offsets)
    any_space = pl.BlockSpec(memory_space=pl.ANY)
    specs = [any_space] * (len(whole) + len(split))
    if filled is not None:
        specs[filled] = vmem()
    shapes = [jax.ShapeDtypeStruct((neigh,) + a.shape, a.dtype) for a in whole]
    shapes += [jax.ShapeDtypeStruct(a.shape, a.dtype) for a in split]
    shapes += [jax.ShapeDtypeStruct((owners,) + spread.shape[-2:], spread.dtype)]

    def kernel(*refs):
        exchange_kernel(owners, offsets, len(whole), len(split), filled, *refs)

    items = (len(whole) + len(split), neigh)
    return pl.pallas_call(
        kernel,
        out_shape=tuple(shapes),
        in_specs=specs + [any_space],
        out_specs=tuple(specs + [any_space]),
        scratch_shapes=[
            pltpu.SemaphoreType.DMA(items),
            pltpu.SemaphoreType.DMA(items),
            pltpu.SemaphoreType.DMA((owners,)),
            pltpu.SemaphoreType.DMA((owners,)),
            pltpu.SemaphoreType.DMA,
            pltpu.SemaphoreType.DMA(items),
        ],
        compiler_params=pltpu.CompilerParams(
            collective_id=ident, has_side_effects=True, vmem_limit_bytes=40 * 1024 * 1024
        ),
        cost_estimate=pl.CostEstimate(flops=0, bytes_accessed=4 * 10**6, transcendentals=0),
        name="exchange",
    )(*whole, *split, spread)


def start_kernel(x_ref, bases_ref, transfers_ref, v_ref, u_ref):
    leaves, _, width = bases_ref.shape
    for leaf in range(leaves):
        v_ref[:, leaf * width : (leaf + 1) * width] = mm(
            transfers_ref[leaf], bases_ref[leaf]
        ).astype(BF16)
    u_ref[...] = mm(x_ref[...], v_ref[...], NT).astype(BF16)


def start_call(x, bases, transfers):
    rank = bases.shape[1]
    return pl.pallas_call(
        start_kernel,
        out_shape=(
            jax.ShapeDtypeStruct((rank, x.shape[1]), BF16),
            jax.ShapeDtypeStruct((x.shape[0], rank), BF16),
        ),
        in_specs=[vmem()] * 3,
        out_specs=(vmem(), vmem()),
        compiler_params=params(),
        cost_estimate=pl.CostEstimate(flops=10**7, bytes_accessed=10**6, transcendentals=0),
        name="parent_basis",
    )(x, bases, transfers)


def local_kernel(unroll, pairs_ref, x_ref, blocks_ref, out_ref, *accs):
    step = pl.program_id(0)
    per_step, width = blocks_ref.shape[0], blocks_ref.shape[1]

    @pl.when(step == 0)
    def _():
        for acc in accs:
            acc[...] = jnp.zeros_like(acc)

    def group(i, carry):
        base = i * unroll
        work = []
        for j in range(unroll):
            place = (step * per_step + base + j) * 2
            target, source = pairs_ref[place], pairs_ref[place + 1]
            block = blocks_ref[base + j]
            work.append(
                (
                    target,
                    source,
                    mm(leaf_cols(x_ref, source, width), block),
                    mm(leaf_cols(x_ref, target, width), block, NT),
                )
            )
        for j, (target, source, to_target, to_source) in enumerate(work):
            first, second = accs[2 * (j % 2)], accs[2 * (j % 2) + 1]
            first[target] += to_target
            second[source] += to_source
        return carry

    lax.fori_loop(0, per_step // unroll, group, 0)

    @pl.when(step == pl.num_programs(0) - 1)
    def _():
        out_ref[...] = (accs[0][...] + accs[1][...]) + (accs[2][...] + accs[3][...])


def local_call(x, pairs, blocks):
    count, width = blocks.shape[0], blocks.shape[1]
    leaves = x.shape[1] // width
    steps = next(s for s in (6, 4, 3, 2, 1) if count % s == 0)
    per_step = count // steps
    unroll = next(s for s in (16, 8, 6, 4, 3, 2, 1) if per_step % s == 0)
    shape = (leaves, x.shape[0], width)

    def kernel(*refs):
        local_kernel(unroll, *refs)

    return pl.pallas_call(
        kernel,
        grid=(steps,),
        out_shape=jax.ShapeDtypeStruct(shape, F32),
        in_specs=[
            smem(),
            vmem(),
            pl.BlockSpec((per_step, width, width), lambda i: (i, 0, 0)),
        ],
        out_specs=vmem(),
        scratch_shapes=[pltpu.VMEM(shape, F32)] * 4,
        compiler_params=params(),
        cost_estimate=pl.CostEstimate(
            flops=count * 4 * 32 * width * width * 16,
            bytes_accessed=blocks.size * 2,
            transcendentals=0,
        ),
        name="local_blocks",
    )(pairs.reshape(-1), x, blocks)


def far_kernel(neigh, cap, slots_ref, back_ref, mine_ref, far_ref, *refs):
    peers, got, ahead_ref, behind_ref = refs
    for k in range(neigh):
        for c in range(cap):
            place = (k * cap + c) * 2
            target = jnp.maximum(slots_ref[place], 0)
            source = jnp.maximum(slots_ref[place + 1], 0)
            lifted = mm(far_ref[k, c], mine_ref[target], TN).astype(BF16)
            ahead_ref[k, c] = mm(peers[k, source], lifted, TN).astype(BF16)
            target = jnp.maximum(back_ref[place], 0)
            source = jnp.maximum(back_ref[place + 1], 0)
            lifted = mm(got[k, c], mine_ref[source]).astype(BF16)
            behind_ref[k, c] = mm(peers[k, target], lifted, TN).astype(BF16)


def far_call(slots, back, bases, blocks, peer_bases, peer_blocks):
    neigh, cap = blocks.shape[0], blocks.shape[1]
    width = bases.shape[2]
    shape = jax.ShapeDtypeStruct((neigh, cap, width, width), BF16)

    def kernel(*refs):
        far_kernel(neigh, cap, *refs)

    return pl.pallas_call(
        kernel,
        out_shape=(shape, shape),
        in_specs=[smem(), smem()] + [vmem()] * 4,
        out_specs=(vmem(), vmem()),
        compiler_params=params(),
        cost_estimate=pl.CostEstimate(flops=10**8, bytes_accessed=4 * 10**6, transcendentals=0),
        name="far_blocks",
    )(slots, back, bases, blocks, peer_bases, peer_blocks)


def join_kernel(
    neigh, near_ref, nback_ref, far_ref, fback_ref, local_ref, v_ref, w_ref, u_ref,
    blocks_ref, ahead_ref, behind_ref, *refs
):
    fields, got, out_ref, next_ref, acc_a, acc_b = refs
    rank = v_ref.shape[0]
    leaves, rows, width = local_ref.shape
    acc_a[:leaves] = local_ref[...]
    acc_b[...] = jnp.zeros_like(acc_b)
    near_cap, far_cap = blocks_ref.shape[1], ahead_ref.shape[1]

    def parent(e, total):
        return total + mm(u_ref[e][:, :rank], w_ref[e])

    total = lax.fori_loop(0, u_ref.shape[0], parent, jnp.zeros((rows, rank), F32))
    down = total.astype(BF16)

    for k in range(neigh):
        work = []
        for c in range(near_cap + far_cap):
            if c < near_cap:
                go, back, place = near_ref, nback_ref, (k * near_cap + c) * 2
                ahead, behind, dims = blocks_ref[k, c], got[k, c], NT
            else:
                go, back, place = far_ref, fback_ref, (k * far_cap + c - near_cap) * 2
                ahead, behind, dims = ahead_ref[k, c - near_cap], behind_ref[k, c - near_cap], NN
            target, source = go[place], go[place + 1]
            there, here = back[place], back[place + 1]
            work.append(
                (
                    jnp.where(target < 0, leaves, target),
                    jnp.where(here < 0, leaves, here),
                    mm(leaf_cols(fields.at[k], jnp.maximum(source, 0), width), ahead),
                    mm(leaf_cols(fields.at[k], jnp.maximum(there, 0), width), behind, dims),
                )
            )
        for target, here, one, two in work:
            acc_a[target] += one
            acc_b[here] += two
    for leaf in range(leaves):
        cols = slice(leaf * width, (leaf + 1) * width)
        out_ref[:, cols] = (acc_a[leaf] + acc_b[leaf] + mm(down, v_ref[:, cols])).astype(BF16)
    next_ref[...] = jnp.zeros_like(next_ref)
    next_ref[:, :rank] = mm(out_ref[...], v_ref[...], NT).astype(BF16)


def join_call(tables, local_sum, v, w, u_all, blocks, far, fields, got):
    neigh = blocks.shape[0]
    leaves, rows, width = local_sum.shape

    def kernel(*refs):
        join_kernel(neigh, *refs)

    return pl.pallas_call(
        kernel,
        out_shape=(
            jax.ShapeDtypeStruct((rows, leaves * width), BF16),
            jax.ShapeDtypeStruct((rows, width), BF16),
        ),
        in_specs=[smem()] * 4 + [vmem()] * 9,
        out_specs=(vmem(), vmem()),
        scratch_shapes=[pltpu.VMEM((leaves + 1, rows, width), F32)] * 2,
        compiler_params=params(),
        cost_estimate=pl.CostEstimate(flops=10**9, bytes_accessed=8 * 10**6, transcendentals=0),
        name="near_and_join",
    )(*tables, local_sum, v, w, u_all, blocks, *far, fields, got)


def exchange_first(owners, offsets, flat, rhs, bases, near, far, spread):
    fields, got_bases, flat_got, got_near, got_far, u_all = exchange_call(
        0, owners, offsets, [rhs, bases], [flat, near, far], spread, filled=2
    )
    return flat_got, fields, got_bases, got_near, got_far, u_all


def body(
    rhs,
    bases,
    transfers,
    near_slots,
    near_blocks,
    local_pairs,
    local_blocks,
    far_slots,
    far_blocks,
    parent_pairs,
    parent_blocks,
):
    neigh = near_slots.shape[1]
    offsets = neighbour_offsets(neigh)
    near, far = near_blocks[0], far_blocks[0]
    near_cap, far_cap = near.shape[1], far.shape[1]

    owners = lax.axis_size("leaf")
    lanes = bases.shape[2]
    slots = jnp.concatenate([near_slots[0], far_slots[0]], axis=1)
    flat = slots.reshape(neigh, 1, -1)
    flat = jnp.pad(flat, ((0, 0), (0, 7), (0, lanes - flat.shape[2])))

    v, u = start_call(rhs, bases, transfers)

    ids = jnp.arange(owners, dtype=jnp.int32)
    live = (parent_pairs[0][:, None] == ids[None, :]).astype(F32)[:, :, None, None]
    parents = parent_blocks[0].astype(F32)
    returned = jnp.sum(live * parents[:, None], axis=0).astype(BF16)
    rank = returned.shape[1]
    spread = jnp.concatenate(
        [
            jnp.broadcast_to(u[None], (owners,) + u.shape),
            returned,
            jnp.zeros((owners, rank, lanes - 2 * rank), BF16),
        ],
        axis=2,
    )
    flat_got, fields, got_bases, got_near, got_far, u_all = exchange_first(
        owners, offsets, flat, rhs, bases, near, far, spread
    )
    back = flat_got[:, 0, : 2 * (near_cap + far_cap)].reshape(neigh, near_cap + far_cap, 2)
    tables = [
        near_slots.reshape(-1),
        back[:, :near_cap].reshape(-1),
        far_slots.reshape(-1),
        back[:, near_cap:].reshape(-1),
    ]
    w = jnp.sum(live * parents.transpose(0, 2, 1)[:, None], axis=0)
    w = (w + u_all[:, :, rank : 2 * rank].astype(F32)).astype(BF16)

    local_sum = local_call(rhs, local_pairs[0], local_blocks[0])
    effective = far_call(tables[2], tables[3], bases, far, got_bases, got_far)
    first, u = join_call(tables, local_sum, v, w, u_all, near, effective, fields, got_near)

    fields, u_all = exchange_call(1, owners, offsets, [first], [], u)
    local_sum = local_call(first, local_pairs[0], local_blocks[0])
    second, _ = join_call(tables, local_sum, v, w, u_all, near, effective, fields, got_near)
    return (first, second)


def solution(mesh):
    in_specs = (
        P("groups", "leaf"),
        P(("groups", "leaf"), None, None),
        P(("groups", "leaf"), None, None),
        P(("groups", "leaf"), None, None, None),
        P(("groups", "leaf"), None, None, None, None),
        P(("groups", "leaf"), None, None),
        P(("groups", "leaf"), None, None, None),
        P(("groups", "leaf"), None, None, None),
        P(("groups", "leaf"), None, None, None, None),
        P(("groups", "leaf"), None),
        P(("groups", "leaf"), None, None, None),
    )
    out_specs = (P("groups", "leaf"), P("groups", "leaf"))
    return jax.shard_map(body, mesh=mesh, in_specs=in_specs, out_specs=out_specs, check_vma=False)
```
